32 devices in a mesh: group: 2 (over y), att: 4 (over z), ffn: 4 (over x, core).
Axes of the slice: x: 2, y: 2, z: 4, core: 2. Of those that a mesh axis runs over, the one named last changes fastest.
Arguments:
- hidden_state: bfloat16 [160, 8192], P(('group', 'att'), 'ffn'), parts along dimension 0, may hold values from -40 to 40
- queries: bfloat16 [160, 8192], P(('group', 'att'), 'ffn'), parts along dimension 0, may hold values from -800 to 800
- key_cache: bfloat16 [102400, 1024], P(('group', 'att'), 'ffn'), parts along dimension 0, may hold values from -6 to 6
- value_cache: bfloat16 [102400, 1024], P(('group', 'att'), 'ffn'), parts along dimension 0, may hold values from -6 to 6
- lengths: int32 [160], P(('group', 'att')), parts along dimension 0, may hold values from 1 to 1279, as said below
- assignment: int32 [160], P('group'), parts along dimension 0, may hold values from 0 to 79, each once
- out_weight: bfloat16 [8, 1024, 8192], P(None, 'att', 'ffn'), may hold values from -0.375 to 0.375
- norm_gain: bfloat16 [8192], P('ffn'), may hold values from 0.099609375 to 1.8984375
- gate_weight: bfloat16 [14336, 8192], P('att', 'ffn'), may hold values from -0.0625 to 0.0625
- up_weight: bfloat16 [14336, 8192], P('att', 'ffn'), may hold values from -0.0625 to 0.0625
- down_weight: bfloat16 [14336, 8192], P('att', 'ffn'), may hold values from -0.0625 to 0.0625
Outputs:
- next_hidden: bfloat16 [160, 8192], P(('group', 'att'), 'ffn'), parts along dimension 0
The draws below stay inside these ranges and needn't reach their ends.
There are 2 independent parts, one for each index of `group`. The reference program is written for one: setup_inputs(seed, part) draws one part's arguments, and reference() takes and returns one part's arrays. A program takes and returns all parts, laid end to end along the dimension named above; an argument that names none is the same for every part. Nothing has to cross between parts.
Inputs may be any that keep to these rules, and one draw needn't show every extreme that they name: Each attention index holds the contexts of its 20 slots end to end in its 12800 cache rows in slot order; their lengths sum to at most 12800, and to exactly 12800 on some attention index in every draw. `assignment`: A permutation of the requests.
All inputs are finite; a program needn't handle non-finite values.
Results may differ from the reference program's by a relative error of at most 0.02.
Values may be sent and summed in bfloat16 or wider, within the bound.
A program may use at most 192 MiB of HBM per device.

```python
import math
import jax
import jax.numpy as jnp
from jax import lax

D = 8192
HQ = 64
KVH = 8
HD = 128
FF = 14336
R_DEV = 20
POOL = 12800
REQS = 80
ROWS = 51200
N_ATT = 4


def draw_lengths(key, part):
    key = jax.random.fold_in(key, 11)
    key_full, key_level, key_pair, key_split, key_order = jax.random.split(key, 5)
    device_count = REQS // R_DEV
    pair_cap = POOL // R_DEV
    pair_count = R_DEV // 2
    full_device = jax.random.randint(key_full, (), 0, device_count)
    device_level = jax.random.randint(key_level, (device_count, 1), max(2, pair_cap // 2), 2 * pair_cap + 1)
    lower_cap = jnp.maximum(2, device_level // 2)
    budget = jax.random.randint(key_pair, (device_count, pair_count), lower_cap, device_level + 1)
    device_rows = jnp.arange(device_count, dtype=jnp.int32)[:, None]
    budget = jnp.where(device_rows == full_device, 2 * pair_cap, budget)
    split_at = jax.random.randint(key_split, (device_count, pair_count), 1, budget)
    lead_pair = jnp.arange(pair_count, dtype=jnp.int32)[None, :] == 0
    split_at = jnp.where((device_rows == full_device) & lead_pair, 1, split_at)
    lengths_grid = jnp.stack([split_at, budget - split_at], axis=-1).reshape(device_count, R_DEV)
    order_keys = jax.random.split(key_order, device_count)
    slot_orders = jax.vmap(lambda order_key: jax.random.permutation(order_key, R_DEV))(order_keys)
    return jnp.take_along_axis(lengths_grid, slot_orders, axis=1).reshape(REQS).astype(jnp.int32)


def draw_hidden_state(key, part):
    key = jax.random.fold_in(key, 21)
    key_entries, key_rows, key_cols = jax.random.split(key, 3)
    column_axis = jnp.arange(D, dtype=jnp.float32) / D
    rough_cols = jnp.exp(jax.random.uniform(key_cols, (D,), minval=math.log(0.7), maxval=math.log(1.4)))
    column_scale = 10.0 ** (column_axis - 0.5) * rough_cols
    entries = jnp.clip(jax.random.normal(key_entries, (REQS, D)), -6.0, 6.0)
    row_scale = jnp.exp(jax.random.uniform(key_rows, (REQS, 1), minval=math.log(0.4), maxval=math.log(4.0)))
    return (0.3 * entries * row_scale * column_scale).astype(jnp.bfloat16)


def draw_queries(key, part):
    key = jax.random.fold_in(key, 31)
    key_entries = jax.random.fold_in(key, 0)
    entries = jnp.clip(jax.random.normal(key_entries, (REQS, HQ, HD)), -6.0, 6.0)
    return entries.reshape(REQS, HQ * HD).astype(jnp.bfloat16)


def draw_key_cache(key, part):
    key = jax.random.fold_in(key, 41)
    key_entries = jax.random.fold_in(key, 0)
    cache_rows = POOL * (REQS // R_DEV)
    entries = jnp.clip(jax.random.normal(key_entries, (cache_rows, KVH, HD)), -6.0, 6.0)
    return entries.reshape(cache_rows, KVH * HD).astype(jnp.bfloat16)


def raised(values, rng, source, target, blocks, factor):
    owner, partner = [(jnp.arange(values.shape[dim]) // (values.shape[dim] // blocks)).reshape([-1 if axis == dim else 1 for axis in range(values.ndim)]) for dim in (source, target)]
    chosen = jax.random.permutation(rng, blocks)[partner]
    strong = (owner == chosen) | (owner == (partner + blocks // 2) % blocks)
    return jnp.where(strong, factor * values, values)


def block_scale(rng, dims, shards, least, largest):
    gain = 1.0
    for axis_at, parts in shards:
        steps = jax.random.uniform(jax.random.fold_in(jax.random.fold_in(rng, 6), axis_at), (parts,), jnp.float32, least / len(shards), largest / len(shards))
        gain = gain * jnp.repeat(jnp.exp(steps), dims[axis_at] // parts).reshape((-1,) + (1,) * (len(dims) - 1 - axis_at))
    return gain


def normal_values(key, dims, width, most, cuts=(), kind=jnp.bfloat16):
    result = jax.random.normal(key, dims, jnp.float32) * width
    if len(cuts) > 0:
        result = block_scale(key, dims, cuts, -0.22, 0.18) * result
    return jnp.clip(result, min=-most, max=most).astype(kind)


def noise_with(key, extent, spread, limit, cuts, heavy, kind=jnp.bfloat16):
    array = spread * jax.random.normal(key, extent, jnp.float32)
    if cuts:
        array = array * block_scale(key, extent, cuts, -0.22, 0.18)
    return jnp.clip(raised(array, jax.random.fold_in(key, 3), *heavy), -limit, limit).astype(kind)


def setup_inputs(seed: int = 0, part: int = 0) -> dict:
    key_of = jax.random.split(jax.random.key(seed), 12)
    own_keys = jax.random.split(jax.random.fold_in(key_of[11], part), 12)
    hidden_state = draw_hidden_state(jax.random.fold_in(jax.random.fold_in(key_of[11], part), 71), part)
    queries = draw_queries(jax.random.fold_in(jax.random.fold_in(key_of[11], part), 71), part)
    key_cache = draw_key_cache(jax.random.fold_in(jax.random.fold_in(key_of[11], part), 71), part)
    value_cache = normal_values(own_keys[3], (ROWS, KVH * HD), 1.0, 6.0, ((0, 4), (1, 4)))
    lengths = draw_lengths(jax.random.fold_in(jax.random.fold_in(key_of[11], part), 71), part)
    assignment = jax.random.permutation(own_keys[5], REQS).astype(jnp.int32)
    out_weight = normal_values(key_of[6], (KVH, HQ // KVH * HD, D), (2 * HD) ** -0.5, 0.375, ((1, 4), (2, 4)))
    norm_gain = jnp.clip(1.0 + 0.18 * jax.random.normal(key_of[7], (D,), jnp.float32), 0.099609375, 1.8984375).astype(jnp.bfloat16)
    gate_weight = normal_values(key_of[8], (FF, D), D ** -0.5, 0.0625, ((0, 4), (1, 4)))
    up_weight = normal_values(key_of[9], (FF, D), D ** -0.5, 0.0625, ((0, 4), (1, 4)))
    down_weight = noise_with(key_of[10], (FF, D), FF ** -0.5, 0.0625, ((0, 4), (1, 4)), (0, 1, 4, 2.0))
    return dict(hidden_state=hidden_state, queries=queries, key_cache=key_cache, value_cache=value_cache, lengths=lengths, assignment=assignment, out_weight=out_weight, norm_gain=norm_gain, gate_weight=gate_weight, up_weight=up_weight, down_weight=down_weight)


epsilon = 1e-05
masked_score = -1e+30

def attend_device(inputs):
    dev_queries, dev_keys, dev_values, dev_lengths = inputs
    slot_starts = jnp.cumsum(dev_lengths) - dev_lengths
    slot_ends = slot_starts + dev_lengths
    positions = jnp.arange(POOL, dtype=jnp.int32)
    owned_rows = (positions[None, :] >= slot_starts[:, None]) & (positions[None, :] < slot_ends[:, None])
    scores = jnp.einsum('rkgc,pkc->rkgp', dev_queries.astype(jnp.float32), dev_keys.astype(jnp.float32))
    scores = scores * (1.0 / jnp.sqrt(jnp.float32(HD)))
    scores = jnp.where(owned_rows[:, None, None, :], scores, masked_score)
    row_top = lax.optimization_barrier(jnp.max(scores, axis=-1, keepdims=True))
    shifted = jnp.exp(scores - row_top)
    totals = lax.optimization_barrier(jnp.sum(shifted, axis=-1, keepdims=True))
    weights = (shifted / totals).astype(jnp.bfloat16)
    attended = jnp.einsum('rkgp,pkc->rkgc', weights.astype(jnp.float32), dev_values.astype(jnp.float32))
    return attended.astype(jnp.bfloat16)

def reference(hidden_state, queries, key_cache, value_cache, lengths, assignment, out_weight, norm_gain, gate_weight, up_weight, down_weight):
    per_group = HQ // KVH
    slot_queries = jnp.take(queries, assignment, axis=0).reshape(N_ATT, R_DEV, KVH, per_group, HD)
    keys_grid = key_cache.reshape(N_ATT, POOL, KVH, HD)
    values_grid = value_cache.reshape(N_ATT, POOL, KVH, HD)
    lengths_grid = lengths.reshape(N_ATT, R_DEV)
    attended = lax.map(attend_device, (slot_queries, keys_grid, values_grid, lengths_grid))
    attended = attended.reshape(REQS, HQ * HD)
    inverse = jnp.zeros((REQS,), jnp.int32).at[assignment].set(jnp.arange(REQS, dtype=jnp.int32))
    request_heads = jnp.take(attended, inverse, axis=0)
    projected = jnp.dot(request_heads, out_weight.reshape(HQ * HD, D), preferred_element_type=jnp.float32)
    middle_short = (hidden_state.astype(jnp.float32) + projected).astype(jnp.bfloat16)
    middle = lax.optimization_barrier(middle_short).astype(jnp.float32)
    squares = lax.optimization_barrier(jnp.sum(middle * middle, axis=1, keepdims=True))
    normed = (middle * lax.rsqrt(squares / D + epsilon) * norm_gain.astype(jnp.float32)).astype(jnp.bfloat16)
    contract = (((1,), (1,)), ((), ()))
    gate_values = lax.dot_general(normed, gate_weight, contract, preferred_element_type=jnp.float32)
    upward = lax.dot_general(normed, up_weight, contract, preferred_element_type=jnp.float32)
    active = (jax.nn.silu(gate_values) * upward).astype(jnp.bfloat16)
    down_values = jnp.dot(active, down_weight, preferred_element_type=jnp.float32)
    return (middle + down_values).astype(jnp.bfloat16)
```

```python
import functools
import math

import jax
import jax.numpy as jnp
from jax import lax
from jax.experimental import pallas as pl
from jax.experimental.pallas import tpu as pltpu
from jax.sharding import PartitionSpec as P

epsilon = 1e-05
masked_score = -1e30


def softmax_rounded(scores):
    row_top = jnp.max(scores, axis=-1, keepdims=True)
    shifted = jnp.exp(scores - row_top)
    totals = jnp.sum(shifted, axis=-1, keepdims=True)
    return (shifted / totals).astype(jnp.bfloat16)


def per_device(
    hidden_state,
    queries,
    key_cache,
    value_cache,
    lengths,
    assignment,
    out_weight,
    norm_gain,
    gate_weight,
    up_weight,
    down_weight,
):
    rows_dev = hidden_state.shape[0]
    columns = hidden_state.shape[1]
    att_count = lax.axis_size("att")
    ffn_count = lax.axis_size("ffn")
    requests = rows_dev * att_count
    kv_total = out_weight.shape[0]
    kv_local = kv_total // ffn_count
    model_width = columns * ffn_count
    pool_rows = key_cache.shape[0]
    head_size = key_cache.shape[1] // kv_local
    per_group = queries.shape[1] // (kv_local * head_size)
    score_scale = 1.0 / math.sqrt(head_size)
    att_place = lax.axis_index("att")
    every_query = lax.all_gather(queries, "att", axis=0, tiled=True)
    own_slots = lax.dynamic_slice_in_dim(assignment, att_place * rows_dev, rows_dev)
    chosen = (own_slots[:, None] == jnp.arange(requests, dtype=jnp.int32)).astype(jnp.bfloat16)
    slot_queries = (chosen @ every_query).reshape(
        rows_dev, kv_local, per_group, head_size
    )
    keys_local = key_cache.reshape(pool_rows, kv_local, head_size)
    values_local = value_cache.reshape(pool_rows, kv_local, head_size)
    slots = jnp.arange(rows_dev, dtype=jnp.int32)
    slot_starts = jnp.sum(jnp.where(slots[None, :] < slots[:, None], lengths[None, :], 0), axis=1)
    slot_ends = slot_starts + lengths
    positions = jnp.arange(pool_rows, dtype=jnp.int32)
    owned_rows = (positions[None, :] >= slot_starts[:, None]) & (
        positions[None, :] < slot_ends[:, None]
    )
    owned_rows = owned_rows[:, None, None, :]
    raw_scores = (
        jnp.einsum("rkgc,pkc->rkgp", slot_queries, keys_local, preferred_element_type=jnp.float32)
        * score_scale
    )
    weights = softmax_rounded(jnp.where(owned_rows, raw_scores, masked_score))
    attended = jnp.einsum(
        "rkgp,pkc->rkgc", weights, values_local, preferred_element_type=jnp.float32
    )
    attended = attended.astype(jnp.bfloat16).reshape(rows_dev, kv_local, per_group * head_size)
    spread = lax.all_to_all(attended, "att", split_axis=2, concat_axis=0, tiled=True)
    pieces = lax.all_gather(spread, "ffn", axis=1, tiled=True)
    placed = (jnp.arange(requests, dtype=jnp.int32)[:, None] == assignment).astype(jnp.bfloat16)
    request_pieces = (placed @ pieces.reshape(requests, -1)).reshape(pieces.shape)
    block = request_pieces
    projected = lax.psum_scatter(
        jnp.einsum("rkc,kcd->rd", block, out_weight, preferred_element_type=jnp.float32).astype(
            jnp.bfloat16
        ),
        "att",
        scatter_dimension=0,
        tiled=True,
    ).astype(jnp.float32)
    middle_short = (hidden_state.astype(jnp.float32) + projected).astype(jnp.bfloat16)
    middle = lax.optimization_barrier(middle_short).astype(jnp.float32)
    squares = lax.psum(jnp.sum(middle * middle, axis=1), "ffn")
    normed = (
        middle * lax.rsqrt(squares[:, None] / model_width + epsilon) * norm_gain.astype(jnp.float32)
    ).astype(jnp.bfloat16)
    every_row = lax.all_gather(normed, "att", axis=0, tiled=True)
    contract = (((1,), (1,)), ((), ()))
    gate_part = lax.dot_general(
        gate_weight, every_row, contract, preferred_element_type=jnp.float32
    )
    up_part = lax.dot_general(up_weight, every_row, contract, preferred_element_type=jnp.float32)
    totals = lax.psum(
        jnp.concatenate([gate_part, up_part], axis=1).astype(jnp.bfloat16), "ffn"
    ).astype(jnp.float32)
    unit_active = (jax.nn.silu(totals[:, :requests]) * totals[:, requests:]).astype(jnp.bfloat16)
    block = unit_active
    returned = lax.psum_scatter(
        lax.dot_general(
            block, down_weight, (((0,), (0,)), ((), ())), preferred_element_type=jnp.float32
        ).astype(jnp.bfloat16),
        "att",
        scatter_dimension=0,
        tiled=True,
    ).astype(jnp.float32)
    return (middle + returned).astype(jnp.bfloat16)


MESH = pl.DeviceIdType.MESH
NT = (((1,), (1,)), ((), ()))


def flip(index, bits):
    result, bit = index, 1
    while bit <= bits:
        if bits & bit:
            result = result + bit - 2 * bit * ((index // bit) % 2)
        bit *= 2
    return result


def tile_of(total, most):
    tile = most - most % 128
    while total % tile:
        tile -= 128
    return tile


def one_hot(targets, width):
    lanes = lax.broadcasted_iota(jnp.int32, (targets.shape[0], width), 1)
    return (lanes == targets).astype(jnp.bfloat16)


def pick(targets, table):
    return jnp.dot(
        one_hot(targets, table.shape[0]), table, preferred_element_type=jnp.float32
    ).astype(jnp.bfloat16)


def layer_kernel(
    sizes,
    places,
    query_ref,
    hidden_ref,
    gain_ref,
    index_ref,
    key_hbm,
    value_hbm,
    out_hbm,
    gate_hbm,
    up_hbm,
    down_hbm,
    result_ref,
    keys,
    values,
    out_w,
    gate_w,
    up_w,
    every_query,
    spread_out,
    spread_in,
    pieces,
    blocks,
    part_out,
    part_in,
    middle,
    every_row,
    rows,
    sq_own,
    sq_in,
    sq_total,
    sq_all,
    gu_out,
    gu_in,
    active,
    load_sem,
    gu_load_sem,
    down_sem,
    att_send,
    att_recv,
    ffn_send,
    ffn_recv,
    part_send,
    part_recv,
    last_send,
    last_recv,
):
    n_att, n_ffn, rows_dev, pad, kv_local, per_group, head = sizes
    att = lax.axis_index("att")
    ffn = lax.axis_index("ffn")
    requests = n_att * rows_dev
    columns = out_w.shape[1]
    model_width = columns * n_ffn
    units = gate_w.shape[0] // n_ffn
    bf16, f32 = jnp.bfloat16, jnp.float32

    def ix(name):
        at, count = places[name]
        return index_ref[:count, at : at + 1]

    key_load = pltpu.make_async_copy(key_hbm, keys, load_sem.at[0])
    value_load = pltpu.make_async_copy(value_hbm, values, load_sem.at[1])
    key_load.start()
    value_load.start()
    kv_total, group_rows = out_hbm.shape[0], out_hbm.shape[1]
    out_loads = [
        pltpu.make_async_copy(
            out_hbm.at[k], out_w.at[pl.ds(k * group_rows, group_rows), :], load_sem.at[2 + k]
        )
        for k in range(kv_total)
    ]
    for copy in out_loads:
        copy.start()
    order = list(range(n_ffn - 1, -1, -1))
    unit_rows = [pl.ds(pl.multiple_of(flip(ffn, d) * units, units), units) for d in range(n_ffn)]
    gu_loads = {}
    for d in order:
        gu_loads[d] = [
            pltpu.make_async_copy(
                source.at[unit_rows[d], :], target.at[unit_rows[d], :], gu_load_sem.at[n, d]
            )
            for n, (source, target) in enumerate(((gate_hbm, gate_w), (up_hbm, up_w)))
        ]
        for copy in gu_loads[d]:
            copy.start()

    att_peer = [lax.rem(att + d, n_att) for d in range(n_att)]
    ffn_peer = [flip(ffn, d) for d in range(n_ffn)]
    barrier = pltpu.get_barrier_semaphore()
    for d in range(1, n_att):
        pl.semaphore_signal(barrier, inc=1, device_id={"att": att_peer[d]}, device_id_type=MESH)
    for d in range(1, n_ffn):
        pl.semaphore_signal(barrier, inc=1, device_id={"ffn": ffn_peer[d]}, device_id_type=MESH)
    pl.semaphore_wait(barrier, n_att + n_ffn - 2)

    def to_att(phase, d, source, target):
        copy = pltpu.make_async_remote_copy(
            src_ref=source,
            dst_ref=target,
            send_sem=att_send.at[phase, d - 1],
            recv_sem=att_recv.at[phase, d - 1],
            device_id={"att": att_peer[d]},
            device_id_type=MESH,
        )
        copy.start()
        return copy

    def to_ffn(phase, d, source, target):
        copy = pltpu.make_async_remote_copy(
            src_ref=source,
            dst_ref=target,
            send_sem=ffn_send.at[phase, d - 1],
            recv_sem=ffn_recv.at[phase, d - 1],
            device_id={"ffn": ffn_peer[d]},
            device_id_type=MESH,
        )
        copy.start()
        return copy

    sent = []
    every_query_copies = [
        to_att(0, d, query_ref, every_query.at[att]) for d in range(1, n_att)
    ]
    every_query[pl.ds(att, 1)] = query_ref[...][None]
    for copy in every_query_copies:
        copy.wait()
    query_table = every_query[...].reshape(-1, head)
    slot_rows = rows_dev * per_group
    query_at = ix("query")
    slot_query = [
        pick(query_at[k * slot_rows : (k + 1) * slot_rows], query_table) for k in range(kv_local)
    ]

    first, count = ix("first"), ix("count")
    pool = keys.shape[0]
    block = tile_of(pool, 512)
    scale = 1.0 / math.sqrt(head)
    key_load.wait()
    value_load.wait()

    def attend(step, carry):
        at = pl.multiple_of(step * block, block)
        spot = lax.broadcasted_iota(jnp.int32, (slot_rows, block), 1) + (at - first)
        owned = (spot >= 0) & (spot < count)
        new = []
        for k in range(kv_local):
            top, total, out = carry[k]
            lanes = slice(k * head, (k + 1) * head)
            scores = lax.dot_general(
                slot_query[k],
                keys[pl.ds(at, block), lanes],
                NT,
                preferred_element_type=f32,
            )
            scores = jnp.where(owned, scores * scale, -1e30)
            new_top = jnp.maximum(top, jnp.max(scores, axis=1, keepdims=True))
            shifted = jnp.where(owned, jnp.exp(scores - new_top), 0.0)
            keep = jnp.exp(top - new_top)
            total = total * keep + jnp.sum(shifted, axis=1, keepdims=True)
            out = out * keep + jnp.dot(
                shifted.astype(bf16), values[pl.ds(at, block), lanes], preferred_element_type=f32
            )
            new.append((new_top, total, out))
        return tuple(new)

    start = tuple(
        (
            jnp.full((slot_rows, 1), -1e30, f32),
            jnp.zeros((slot_rows, 1), f32),
            jnp.zeros((slot_rows, head), f32),
        )
        for _ in range(kv_local)
    )
    finished = lax.fori_loop(0, pool // block, attend, start)
    attended = jnp.concatenate([(out / total).astype(bf16) for _, total, out in finished], axis=0)

    spread_out[...] = pick(ix("spread"), attended).reshape(spread_out.shape)
    spread_copies = [
        to_att(1, d, spread_out.at[att_peer[d]], spread_in.at[att]) for d in range(1, n_att)
    ]
    spread_in[pl.ds(att, 1)] = spread_out[pl.ds(att, 1)]
    for copy in spread_copies:
        copy.wait()
    piece_copies = [to_ffn(0, d, spread_in, pieces.at[ffn]) for d in range(1, n_ffn)]
    pieces[pl.ds(ffn, 1)] = spread_in[...][None]
    for copy in piece_copies:
        copy.wait()

    table = jnp.concatenate(
        [pieces[f].reshape(-1, head) for f in range(n_ffn)], axis=1
    )
    padded = n_att * pad
    request_at = ix("request")
    parts_kv = request_at.shape[0] // padded
    for n in range(parts_kv):
        picked = pick(request_at[n * padded : (n + 1) * padded], table)
        for f in range(n_ffn):
            at = (f * parts_kv + n) * head
            blocks[:, at : at + head] = picked[:, f * head : (f + 1) * head]
    for copy in out_loads:
        copy.wait()

    wide = tile_of(columns, 512)
    chunks = columns // wide

    def to_owner(c, d, out_buf, in_buf, send, recv):
        lanes = pl.ds(c * wide, wide)
        copy = pltpu.make_async_remote_copy(
            src_ref=out_buf.at[att_peer[d], :, lanes],
            dst_ref=in_buf.at[d - 1, :, lanes],
            send_sem=send.at[d - 1, c],
            recv_sem=recv.at[d - 1, c],
            device_id={"att": att_peer[d]},
            device_id_type=MESH,
        )
        copy.start()
        return copy

    owner_copies = []
    for c in range(chunks):
        lanes = slice(c * wide, (c + 1) * wide)
        product = jnp.dot(blocks[...], out_w[:, lanes], preferred_element_type=f32)
        part_out[:, :, lanes] = product.astype(bf16).reshape(n_att, pad, wide)
        owner_copies.append(
            [to_owner(c, d, part_out, part_in, part_send, part_recv) for d in range(1, n_att)]
        )
    squares = jnp.zeros((pad, 1), f32)
    for c in range(chunks):
        lanes = slice(c * wide, (c + 1) * wide)
        for copy in owner_copies[c]:
            copy.wait()
        projected = part_out[pl.ds(att, 1), :, lanes].reshape(pad, wide).astype(f32)
        for d in range(1, n_att):
            projected = projected + part_in[d - 1, :, lanes].astype(f32)
        mid_short = (hidden_ref[:, lanes].astype(f32) + projected).astype(bf16)
        middle[:, lanes] = mid_short
        mid = mid_short.astype(f32)
        squares = squares + jnp.sum(mid * mid, axis=1, keepdims=True)
        every_row[pl.ds(att, 1), :, lanes] = (
            (mid * gain_ref[:, lanes].astype(f32)).astype(bf16)[None]
        )
    row_copies = [
        to_att(2, d, every_row.at[att], every_row.at[att]) for d in range(1, n_att)
    ]
    sq_own[...] = jnp.broadcast_to(squares, sq_own.shape)
    sq_copies = [to_ffn(1, d, sq_own, sq_in.at[d - 1]) for d in range(1, n_ffn)]
    for copy in sq_copies:
        copy.wait()
    whole = sq_own[...]
    for d in range(1, n_ffn):
        whole = whole + sq_in[d - 1]
    sq_total[...] = lax.rsqrt(whole / model_width + epsilon)
    sq_all[pl.ds(att, 1)] = sq_total[...][None]
    scale_copies = [to_att(3, d, sq_total, sq_all.at[att]) for d in range(1, n_att)]
    for copy in row_copies:
        copy.wait()
    row_pick = one_hot(ix("narrow"), padded)
    for c in range(chunks):
        lanes = slice(c * wide, (c + 1) * wide)
        rows[:, lanes] = jnp.dot(
            row_pick, every_row[:, :, lanes].reshape(padded, wide), preferred_element_type=f32
        ).astype(bf16)

    gu_copies = []
    down_loads = []
    own = None
    for d in order:
        for copy in gu_loads[d]:
            copy.wait()
        made = []
        for weight in (gate_w, up_w):
            total = jnp.zeros((requests, units), f32)
            for c in range(chunks):
                lanes = slice(c * wide, (c + 1) * wide)
                total = total + lax.dot_general(
                    rows[:, lanes], weight[unit_rows[d], lanes], NT, preferred_element_type=f32
                )
            made.append(total)
        if d:
            gu_out[d - 1, 0] = made[0].astype(bf16)
            gu_out[d - 1, 1] = made[1].astype(bf16)
            gu_copies.append(to_ffn(2, d, gu_out.at[d - 1], gu_in.at[d - 1]))
        else:
            own = made
        load = pltpu.make_async_copy(
            down_hbm.at[unit_rows[d], :], gate_w.at[unit_rows[d], :], down_sem.at[d]
        )
        load.start()
        down_loads.append(load)
    for copy in scale_copies:
        copy.wait()
    row_scale = jnp.dot(
        row_pick.astype(f32),
        sq_all[...].reshape(padded, sq_all.shape[2]),
        preferred_element_type=f32,
        precision=lax.Precision.HIGHEST,
    )[:, :1]
    gate, upward = own
    for copy in gu_copies:
        copy.wait()
    for d in range(1, n_ffn):
        gate = gate + gu_in[d - 1, 0].astype(f32)
        upward = upward + gu_in[d - 1, 1].astype(f32)
    gate = gate * row_scale
    unit_active = (gate / (1.0 + jnp.exp(-gate)) * (upward * row_scale)).astype(bf16)
    active[pl.ds(ffn, 1)] = unit_active[None]
    active_copies = [
        to_ffn(3, d, active.at[ffn], active.at[ffn]) for d in range(1, n_ffn)
    ]
    for copy in active_copies:
        copy.wait()
    widen = one_hot(ix("widen"), requests)
    for load in down_loads:
        load.wait()

    last_copies = []
    for c in range(chunks):
        lanes = slice(c * wide, (c + 1) * wide)
        product = jnp.dot(active[0], gate_w[:units, lanes], preferred_element_type=f32)
        for f in range(1, n_ffn):
            product = product + jnp.dot(
                active[f], gate_w[f * units : (f + 1) * units, lanes], preferred_element_type=f32
            )
        product = jnp.dot(widen, product.astype(bf16), preferred_element_type=f32)
        part_out[:, :, lanes] = product.astype(bf16).reshape(n_att, pad, wide)
        last_copies.append(
            [to_owner(c, d, part_out, part_in, last_send, last_recv) for d in range(1, n_att)]
        )
    for c in range(chunks):
        lanes = slice(c * wide, (c + 1) * wide)
        for copy in last_copies[c]:
            copy.wait()
        returned = part_out[pl.ds(att, 1), :, lanes].reshape(pad, wide).astype(f32)
        for d in range(1, n_att):
            returned = returned + part_in[d - 1, :, lanes].astype(f32)
        result_ref[:, lanes] = (middle[:, lanes].astype(f32) + returned).astype(bf16)


def fused_device(
    hidden_state,
    queries,
    key_cache,
    value_cache,
    lengths,
    assignment,
    out_weight,
    norm_gain,
    gate_weight,
    up_weight,
    down_weight,
):
    rows_dev, columns = hidden_state.shape
    n_att, n_ffn = lax.axis_size("att"), lax.axis_size("ffn")
    requests = rows_dev * n_att
    kv_total, group_rows, _ = out_weight.shape
    kv_local = kv_total // n_ffn
    head = key_cache.shape[1] // kv_local
    per_group = queries.shape[1] // (kv_local * head)
    heads_here = group_rows // head
    pool = key_cache.shape[0]
    hidden_units = gate_weight.shape[0]
    units = hidden_units // n_ffn
    pad = -(-rows_dev // 16) * 16
    padded = n_att * pad
    i32, bf16, f32 = jnp.int32, jnp.bfloat16, jnp.float32

    own_slots = lax.dynamic_slice_in_dim(assignment, lax.axis_index("att") * rows_dev, rows_dev)
    k_ix = jnp.arange(kv_local, dtype=i32)
    g_ix = jnp.arange(per_group, dtype=i32)
    s_ix = jnp.arange(rows_dev, dtype=i32)
    a_ix = jnp.arange(n_att, dtype=i32)
    h_ix = jnp.arange(heads_here, dtype=i32)
    query_at = (
        own_slots[None, :, None] * (kv_local * per_group)
        + k_ix[:, None, None] * per_group
        + g_ix[None, None, :]
    ).reshape(-1)
    starts = jnp.sum(jnp.where(s_ix[None, :] < s_ix[:, None], lengths[None, :], 0), axis=1)
    first = jnp.repeat(starts, per_group)
    count = jnp.repeat(lengths, per_group)
    spread_at = (
        k_ix[None, :, None, None] * (rows_dev * per_group)
        + s_ix[None, None, None, :] * per_group
        + a_ix[:, None, None, None] * heads_here
        + h_ix[None, None, :, None]
    ).reshape(-1)
    all_ix = jnp.arange(requests, dtype=i32)
    inverse = jnp.sum(
        jnp.where(assignment[None, :] == all_ix[:, None], all_ix[None, :], 0), axis=1
    )
    inverse_pad = jnp.pad(
        inverse.reshape(n_att, rows_dev), ((0, 0), (0, pad - rows_dev)), constant_values=-1
    ).reshape(-1)
    slot_at = (inverse_pad // rows_dev) * (kv_local * heads_here * rows_dev) + inverse_pad % rows_dev
    parts = jnp.arange(kv_local * heads_here, dtype=i32)
    request_at = jnp.where(
        inverse_pad[None, :] >= 0, slot_at[None, :] + parts[:, None] * rows_dev, -1
    ).reshape(-1)
    narrow_at = (a_ix[:, None] * pad + s_ix[None, :]).reshape(-1)
    p_ix = jnp.arange(pad, dtype=i32)
    widen_at = jnp.where(
        p_ix[None, :] < rows_dev, a_ix[:, None] * rows_dev + p_ix[None, :], -1
    ).reshape(-1)
    named = [
        ("query", query_at),
        ("first", first),
        ("count", count),
        ("spread", spread_at),
        ("request", request_at),
        ("narrow", narrow_at),
        ("widen", widen_at),
    ]
    longest = max(array.shape[0] for _, array in named)
    places = {name: (n, array.shape[0]) for n, (name, array) in enumerate(named)}
    index = jnp.stack([jnp.pad(array, (0, longest - array.shape[0])) for _, array in named], axis=1)

    query_rows = queries.reshape(-1, head)
    hidden_pad = jnp.pad(hidden_state, ((0, pad - rows_dev), (0, 0)))
    piece_rows = kv_local * heads_here * rows_dev
    wide = tile_of(columns, 512)
    chunks = columns // wide
    sizes = (n_att, n_ffn, rows_dev, pad, kv_local, per_group, head)
    vmem = pl.BlockSpec(memory_space=pltpu.VMEM)
    hbm = pl.BlockSpec(memory_space=pl.ANY)
    dma = pltpu.SemaphoreType.DMA
    V = pltpu.VMEM
    flops = 2 * requests * columns * (3 * hidden_units + kv_total * group_rows)
    moved = 2 * columns * (3 * hidden_units + kv_total * group_rows) + 4 * key_cache.size
    result = pl.pallas_call(
        functools.partial(layer_kernel, sizes, places),
        out_shape=jax.ShapeDtypeStruct((pad, columns), bf16),
        in_specs=[vmem] * 4 + [hbm] * 6,
        out_specs=vmem,
        scratch_shapes=[
            V(key_cache.shape, bf16),
            V(value_cache.shape, bf16),
            V((kv_total * group_rows, columns), bf16),
            V(gate_weight.shape, bf16),
            V(up_weight.shape, bf16),
            V((n_att,) + query_rows.shape, bf16),
            V((n_att, piece_rows, head), bf16),
            V((n_att, piece_rows, head), bf16),
            V((n_ffn, n_att, piece_rows, head), bf16),
            V((padded, kv_total * group_rows), bf16),
            V((n_att, pad, columns), bf16),
            V((n_att - 1, pad, columns), bf16),
            V((pad, columns), bf16),
            V((n_att, pad, columns), bf16),
            V((requests, columns), bf16),
            V((pad, 128), f32),
            V((n_ffn - 1, pad, 128), f32),
            V((pad, 128), f32),
            V((n_att, pad, 128), f32),
            V((n_ffn - 1, 2, requests, units), bf16),
            V((n_ffn - 1, 2, requests, units), bf16),
            V((n_ffn, requests, units), bf16),
            dma((2 + kv_total,)),
            dma((2, n_ffn)),
            dma((n_ffn,)),
            dma((4, n_att - 1)),
            dma((4, n_att - 1)),
            dma((4, n_ffn - 1)),
            dma((4, n_ffn - 1)),
            dma((n_att - 1, chunks)),
            dma((n_att - 1, chunks)),
            dma((n_att - 1, chunks)),
            dma((n_att - 1, chunks)),
        ],
        compiler_params=pltpu.CompilerParams(
            collective_id=0, has_side_effects=True, vmem_limit_bytes=61 * 2**20
        ),
        cost_estimate=pl.CostEstimate(flops=flops, bytes_accessed=moved, transcendentals=0),
        name="decode_layer",
    )(
        query_rows,
        hidden_pad,
        norm_gain[None, :],
        index,
        key_cache,
        value_cache,
        out_weight,
        gate_weight,
        up_weight,
        down_weight,
    )
    return result[:rows_dev]


def fits_kernel(mesh, out_weight, key_cache, gate_weight):
    n_att, n_ffn = mesh.shape["att"], mesh.shape["ffn"]
    head = key_cache.shape[1] // out_weight.shape[0]
    group_rows = out_weight.shape[1] // n_att
    units = gate_weight.shape[0] // (n_att * n_ffn)
    return n_ffn & (n_ffn - 1) == 0 and group_rows % head == 0 and units % 128 == 0


def solution(mesh):
    in_specs = (
        P(("group", "att"), "ffn"),
        P(("group", "att"), "ffn"),
        P(("group", "att"), "ffn"),
        P(("group", "att"), "ffn"),
        P(("group", "att")),
        P("group"),
        P(None, "att", "ffn"),
        P("ffn"),
        P("att", "ffn"),
        P("att", "ffn"),
        P("att", "ffn"),
    )
    out_specs = P(("group", "att"), "ffn")

    def run(*arrays):
        body = fused_device if fits_kernel(mesh, arrays[6], arrays[2], arrays[8]) else per_device
        return jax.shard_map(
            body, mesh=mesh, in_specs=in_specs, out_specs=out_specs, check_vma=False
        )(*arrays)

    return run
```

```python
import functools
import math

import jax
import jax.numpy as jnp
from jax import lax
from jax.experimental import pallas as pl
from jax.experimental.pallas import tpu as pltpu
from jax.sharding import PartitionSpec as P

epsilon = 1e-05
masked_score = -1e30


def softmax_rounded(scores):
    row_top = jnp.max(scores, axis=-1, keepdims=True)
    shifted = jnp.exp(scores - row_top)
    totals = jnp.sum(shifted, axis=-1, keepdims=True)
    return (shifted / totals).astype(jnp.bfloat16)


def per_device(
    hidden_state,
    queries,
    key_cache,
    value_cache,
    lengths,
    assignment,
    out_weight,
    norm_gain,
    gate_weight,
    up_weight,
    down_weight,
):
    rows_dev = hidden_state.shape[0]
    columns = hidden_state.shape[1]
    att_count = lax.axis_size("att")
    ffn_count = lax.axis_size("ffn")
    requests = rows_dev * att_count
    kv_total = out_weight.shape[0]
    kv_local = kv_total // ffn_count
    model_width = columns * ffn_count
    pool_rows = key_cache.shape[0]
    head_size = key_cache.shape[1] // kv_local
    per_group = queries.shape[1] // (kv_local * head_size)
    score_scale = 1.0 / math.sqrt(head_size)
    att_place = lax.axis_index("att")
    every_query = lax.all_gather(queries, "att", axis=0, tiled=True)
    own_slots = lax.dynamic_slice_in_dim(assignment, att_place * rows_dev, rows_dev)
    chosen = (own_slots[:, None] == jnp.arange(requests, dtype=jnp.int32)).astype(jnp.bfloat16)
    slot_queries = (chosen @ every_query).reshape(
        rows_dev, kv_local, per_group, head_size
    )
    keys_local = key_cache.reshape(pool_rows, kv_local, head_size)
    values_local = value_cache.reshape(pool_rows, kv_local, head_size)
    slots = jnp.arange(rows_dev, dtype=jnp.int32)
    slot_starts = jnp.sum(jnp.where(slots[None, :] < slots[:, None], lengths[None, :], 0), axis=1)
    slot_ends = slot_starts + lengths
    positions = jnp.arange(pool_rows, dtype=jnp.int32)
    owned_rows = (positions[None, :] >= slot_starts[:, None]) & (
        positions[None, :] < slot_ends[:, None]
    )
    owned_rows = owned_rows[:, None, None, :]
    raw_scores = (
        jnp.einsum("rkgc,pkc->rkgp", slot_queries, keys_local, preferred_element_type=jnp.float32)
        * score_scale
    )
    weights = softmax_rounded(jnp.where(owned_rows, raw_scores, masked_score))
    attended = jnp.einsum(
        "rkgp,pkc->rkgc", weights, values_local, preferred_element_type=jnp.float32
    )
    attended = attended.astype(jnp.bfloat16).reshape(rows_dev, kv_local, per_group * head_size)
    spread = lax.all_to_all(attended, "att", split_axis=2, concat_axis=0, tiled=True)
    pieces = lax.all_gather(spread, "ffn", axis=1, tiled=True)
    placed = (jnp.arange(requests, dtype=jnp.int32)[:, None] == assignment).astype(jnp.bfloat16)
    request_pieces = (placed @ pieces.reshape(requests, -1)).reshape(pieces.shape)
    block = request_pieces
    projected = lax.psum_scatter(
        jnp.einsum("rkc,kcd->rd", block, out_weight, preferred_element_type=jnp.float32).astype(
            jnp.bfloat16
        ),
        "att",
        scatter_dimension=0,
        tiled=True,
    ).astype(jnp.float32)
    middle_short = (hidden_state.astype(jnp.float32) + projected).astype(jnp.bfloat16)
    middle = lax.optimization_barrier(middle_short).astype(jnp.float32)
    squares = lax.psum(jnp.sum(middle * middle, axis=1), "ffn")
    normed = (
        middle * lax.rsqrt(squares[:, None] / model_width + epsilon) * norm_gain.astype(jnp.float32)
    ).astype(jnp.bfloat16)
    every_row = lax.all_gather(normed, "att", axis=0, tiled=True)
    contract = (((1,), (1,)), ((), ()))
    gate_part = lax.dot_general(
        gate_weight, every_row, contract, preferred_element_type=jnp.float32
    )
    up_part = lax.dot_general(up_weight, every_row, contract, preferred_element_type=jnp.float32)
    totals = lax.psum(
        jnp.concatenate([gate_part, up_part], axis=1).astype(jnp.bfloat16), "ffn"
    ).astype(jnp.float32)
    unit_active = (jax.nn.silu(totals[:, :requests]) * totals[:, requests:]).astype(jnp.bfloat16)
    block = unit_active
    returned = lax.psum_scatter(
        lax.dot_general(
            block, down_weight, (((0,), (0,)), ((), ())), preferred_element_type=jnp.float32
        ).astype(jnp.bfloat16),
        "att",
        scatter_dimension=0,
        tiled=True,
    ).astype(jnp.float32)
    return (middle + returned).astype(jnp.bfloat16)


MESH = pl.DeviceIdType.MESH
NT = (((1,), (1,)), ((), ()))


def flip(index, bits):
    result, bit = index, 1
    while bit <= bits:
        if bits & bit:
            result = result + bit - 2 * bit * ((index // bit) % 2)
        bit *= 2
    return result


def tile_of(total, most):
    tile = most - most % 128
    while total % tile:
        tile -= 128
    return tile


def one_hot(targets, width):
    lanes = lax.broadcasted_iota(jnp.int32, (targets.shape[0], width), 1)
    return (lanes == targets).astype(jnp.bfloat16)


def pick(targets, table):
    return jnp.dot(
        one_hot(targets, table.shape[0]), table, preferred_element_type=jnp.float32
    ).astype(jnp.bfloat16)


def layer_kernel(
    sizes,
    places,
    query_ref,
    hidden_ref,
    gain_ref,
    index_ref,
    key_hbm,
    value_hbm,
    out_hbm,
    gate_hbm,
    up_hbm,
    down_hbm,
    result_ref,
    keys,
    values,
    out_w,
    gate_w,
    up_w,
    every_query,
    spread_out,
    spread_in,
    pieces,
    blocks,
    part_out,
    part_in,
    middle,
    every_row,
    rows,
    sq_own,
    sq_in,
    sq_total,
    sq_all,
    gu_out,
    gu_in,
    active,
    down_sum,
    load_sem,
    gu_load_sem,
    down_sem,
    att_send,
    att_recv,
    ffn_send,
    ffn_recv,
    part_send,
    part_recv,
    last_send,
    last_recv,
):
    n_att, n_ffn, rows_dev, pad, kv_local, per_group, head = sizes
    att = lax.axis_index("att")
    ffn = lax.axis_index("ffn")
    requests = n_att * rows_dev
    columns = out_w.shape[1]
    model_width = columns * n_ffn
    units = gate_w.shape[0] // n_ffn
    bf16, f32 = jnp.bfloat16, jnp.float32

    def ix(name):
        at, count = places[name]
        return index_ref[:count, at : at + 1]

    key_load = pltpu.make_async_copy(key_hbm, keys, load_sem.at[0])
    value_load = pltpu.make_async_copy(value_hbm, values, load_sem.at[1])
    key_load.start()
    value_load.start()
    kv_total, group_rows = out_hbm.shape[0], out_hbm.shape[1]
    out_loads = [
        pltpu.make_async_copy(
            out_hbm.at[k], out_w.at[pl.ds(k * group_rows, group_rows), :], load_sem.at[2 + k]
        )
        for k in range(kv_total)
    ]
    for copy in out_loads:
        copy.start()
    order = list(range(n_ffn - 1, -1, -1))
    unit_rows = [pl.ds(pl.multiple_of(flip(ffn, d) * units, units), units) for d in range(n_ffn)]
    gu_loads = {}
    for d in order:
        gu_loads[d] = [
            pltpu.make_async_copy(
                source.at[unit_rows[d], :], target.at[unit_rows[d], :], gu_load_sem.at[n, d]
            )
            for n, (source, target) in enumerate(((gate_hbm, gate_w), (up_hbm, up_w)))
        ]
        for copy in gu_loads[d]:
            copy.start()

    att_peer = [lax.rem(att + d, n_att) for d in range(n_att)]
    ffn_peer = [flip(ffn, d) for d in range(n_ffn)]
    barrier = pltpu.get_barrier_semaphore()
    for d in range(1, n_att):
        pl.semaphore_signal(barrier, inc=1, device_id={"att": att_peer[d]}, device_id_type=MESH)
    for d in range(1, n_ffn):
        pl.semaphore_signal(barrier, inc=1, device_id={"ffn": ffn_peer[d]}, device_id_type=MESH)
    pl.semaphore_wait(barrier, n_att + n_ffn - 2)

    def to_att(phase, d, source, target):
        copy = pltpu.make_async_remote_copy(
            src_ref=source,
            dst_ref=target,
            send_sem=att_send.at[phase, d - 1],
            recv_sem=att_recv.at[phase, d - 1],
            device_id={"att": att_peer[d]},
            device_id_type=MESH,
        )
        copy.start()
        return copy

    def to_ffn(phase, d, source, target):
        copy = pltpu.make_async_remote_copy(
            src_ref=source,
            dst_ref=target,
            send_sem=ffn_send.at[phase, d - 1],
            recv_sem=ffn_recv.at[phase, d - 1],
            device_id={"ffn": ffn_peer[d]},
            device_id_type=MESH,
        )
        copy.start()
        return copy

    sent = []
    every_query_copies = [
        to_att(0, d, query_ref, every_query.at[att]) for d in range(1, n_att)
    ]
    every_query[pl.ds(att, 1)] = query_ref[...][None]
    for copy in every_query_copies:
        copy.wait()
    query_table = every_query[...].reshape(-1, head)
    slot_rows = rows_dev * per_group
    query_at = ix("query")
    slot_query = [
        pick(query_at[k * slot_rows : (k + 1) * slot_rows], query_table) for k in range(kv_local)
    ]

    first, count = ix("first"), ix("count")
    pool = keys.shape[0]
    block = tile_of(pool, 1280)
    scale = 1.0 / (math.sqrt(head) * math.log(2.0))
    key_load.wait()
    value_load.wait()

    def attend(step, carry):
        at = pl.multiple_of(step * block, block)
        spot = lax.broadcasted_iota(jnp.int32, (slot_rows, block), 1) + (at - first)
        owned = (spot >= 0) & (spot < count)
        new = []
        for k in range(kv_local):
            top, total, out = carry[k]
            lanes = slice(k * head, (k + 1) * head)
            scores = lax.dot_general(
                slot_query[k],
                keys[pl.ds(at, block), lanes],
                NT,
                preferred_element_type=f32,
            )
            scores = jnp.where(owned, scores, -1e30)
            new_top = jnp.maximum(top, jnp.max(scores, axis=1, keepdims=True))
            shifted = jnp.exp2((scores - new_top) * scale)
            keep = jnp.exp2((top - new_top) * scale)
            total = total * keep + jnp.sum(shifted, axis=1, keepdims=True)
            out = out * keep + jnp.dot(
                shifted.astype(bf16), values[pl.ds(at, block), lanes], preferred_element_type=f32
            )
            new.append((new_top, total, out))
        return tuple(new)

    start = tuple(
        (
            jnp.full((slot_rows, 1), -1e30, f32),
            jnp.zeros((slot_rows, 1), f32),
            jnp.zeros((slot_rows, head), f32),
        )
        for _ in range(kv_local)
    )
    finished = lax.fori_loop(0, pool // block, attend, start)
    attended = jnp.concatenate([(out / total).astype(bf16) for _, total, out in finished], axis=0)

    spread_out[...] = pick(ix("spread"), attended).reshape(spread_out.shape)
    spread_copies = [
        to_att(1, d, spread_out.at[att_peer[d]], spread_in.at[att]) for d in range(1, n_att)
    ]
    spread_in[pl.ds(att, 1)] = spread_out[pl.ds(att, 1)]
    for copy in spread_copies:
        copy.wait()
    piece_copies = [to_ffn(0, d, spread_in, pieces.at[ffn]) for d in range(1, n_ffn)]
    pieces[pl.ds(ffn, 1)] = spread_in[...][None]
    for copy in piece_copies:
        copy.wait()

    table = jnp.concatenate(
        [pieces[f].reshape(-1, head) for f in range(n_ffn)], axis=1
    )
    padded = n_att * pad
    request_at = ix("request")
    parts_kv = request_at.shape[0] // padded
    for n in range(parts_kv):
        picked = pick(request_at[n * padded : (n + 1) * padded], table)
        for f in range(n_ffn):
            at = (f * parts_kv + n) * head
            blocks[:, at : at + head] = picked[:, f * head : (f + 1) * head]
    for copy in out_loads:
        copy.wait()

    wide = tile_of(columns, 512)
    chunks = columns // wide

    def to_owner(c, d, out_buf, in_buf, send, recv):
        lanes = pl.ds(c * wide, wide)
        copy = pltpu.make_async_remote_copy(
            src_ref=out_buf.at[att_peer[d], :, lanes],
            dst_ref=in_buf.at[d - 1, :, lanes],
            send_sem=send.at[d - 1, c],
            recv_sem=recv.at[d - 1, c],
            device_id={"att": att_peer[d]},
            device_id_type=MESH,
        )
        copy.start()
        return copy

    owner_copies = []
    for c in range(chunks):
        lanes = slice(c * wide, (c + 1) * wide)
        product = jnp.dot(blocks[...], out_w[:, lanes], preferred_element_type=f32)
        part_out[:, :, lanes] = product.astype(bf16).reshape(n_att, pad, wide)
        owner_copies.append(
            [to_owner(c, d, part_out, part_in, part_send, part_recv) for d in range(1, n_att)]
        )
    squares = jnp.zeros((pad, 1), f32)
    for c in range(chunks):
        lanes = slice(c * wide, (c + 1) * wide)
        for copy in owner_copies[c]:
            copy.wait()
        projected = part_out[pl.ds(att, 1), :, lanes].reshape(pad, wide).astype(f32)
        for d in range(1, n_att):
            projected = projected + part_in[d - 1, :, lanes].astype(f32)
        mid_short = (hidden_ref[:, lanes].astype(f32) + projected).astype(bf16)
        middle[:, lanes] = mid_short
        mid = mid_short.astype(f32)
        squares = squares + jnp.sum(mid * mid, axis=1, keepdims=True)
        every_row[pl.ds(att, 1), :, lanes] = (
            (mid * gain_ref[:, lanes].astype(f32)).astype(bf16)[None]
        )
    row_copies = [
        to_att(2, d, every_row.at[att], every_row.at[att]) for d in range(1, n_att)
    ]
    sq_own[...] = jnp.broadcast_to(squares, sq_own.shape)
    sq_copies = [to_ffn(1, d, sq_own, sq_in.at[d - 1]) for d in range(1, n_ffn)]
    for copy in sq_copies:
        copy.wait()
    whole = sq_own[...]
    for d in range(1, n_ffn):
        whole = whole + sq_in[d - 1]
    sq_total[...] = lax.rsqrt(whole / model_width + epsilon)
    sq_all[pl.ds(att, 1)] = sq_total[...][None]
    scale_copies = [to_att(3, d, sq_total, sq_all.at[att]) for d in range(1, n_att)]
    for copy in row_copies:
        copy.wait()
    row_pick = one_hot(ix("narrow"), padded)
    for c in range(chunks):
        lanes = slice(c * wide, (c + 1) * wide)
        rows[:, lanes] = jnp.dot(
            row_pick, every_row[:, :, lanes].reshape(padded, wide), preferred_element_type=f32
        ).astype(bf16)

    gu_copies = []
    down_loads = []
    own = None
    for d in order:
        for copy in gu_loads[d]:
            copy.wait()
        made = []
        for weight in (gate_w, up_w):
            total = jnp.zeros((requests, units), f32)
            for c in range(chunks):
                lanes = slice(c * wide, (c + 1) * wide)
                total = total + lax.dot_general(
                    rows[:, lanes], weight[unit_rows[d], lanes], NT, preferred_element_type=f32
                )
            made.append(total)
        if d:
            gu_out[d - 1, 0] = made[0].astype(bf16)
            gu_out[d - 1, 1] = made[1].astype(bf16)
            gu_copies.append(to_ffn(2, d, gu_out.at[d - 1], gu_in.at[d - 1]))
        else:
            own = made
        load = pltpu.make_async_copy(
            down_hbm.at[unit_rows[d], :], gate_w.at[unit_rows[d], :], down_sem.at[d]
        )
        load.start()
        down_loads.append(load)
    for copy in scale_copies:
        copy.wait()
    row_scale = jnp.dot(
        row_pick.astype(f32),
        sq_all[...].reshape(padded, sq_all.shape[2]),
        preferred_element_type=f32,
        precision=lax.Precision.HIGHEST,
    )[:, :1]
    gate, upward = own
    for copy in gu_copies:
        copy.wait()
    for d in range(1, n_ffn):
        gate = gate + gu_in[d - 1, 0].astype(f32)
        upward = upward + gu_in[d - 1, 1].astype(f32)
    gate = gate * row_scale
    unit_active = (gate / (1.0 + jnp.exp(-gate)) * (upward * row_scale)).astype(bf16)
    active[pl.ds(ffn, 1)] = unit_active[None]
    active_copies = [
        to_ffn(3, d, active.at[ffn], active.at[ffn]) for d in range(1, n_ffn)
    ]
    widen = one_hot(ix("widen"), requests)
    last_copies = []
    for d in range(n_ffn):
        if d:
            active_copies[d - 1].wait()
        down_loads[n_ffn - 1 - d].wait()
        arrived = active[pl.ds(ffn_peer[d], 1)].reshape(requests, units)
        for c in range(chunks):
            lanes = slice(c * wide, (c + 1) * wide)
            product = jnp.dot(arrived, gate_w[unit_rows[d], lanes], preferred_element_type=f32)
            if d:
                product = down_sum[:, lanes] + product
            if d < n_ffn - 1:
                down_sum[:, lanes] = product
                continue
            product = jnp.dot(widen, product.astype(bf16), preferred_element_type=f32)
            part_out[:, :, lanes] = product.astype(bf16).reshape(n_att, pad, wide)
            last_copies.append(
                [to_owner(c, d, part_out, part_in, last_send, last_recv) for d in range(1, n_att)]
            )
    for c in range(chunks):
        lanes = slice(c * wide, (c + 1) * wide)
        for copy in last_copies[c]:
            copy.wait()
        returned = part_out[pl.ds(att, 1), :, lanes].reshape(pad, wide).astype(f32)
        for d in range(1, n_att):
            returned = returned + part_in[d - 1, :, lanes].astype(f32)
        result_ref[:, lanes] = (middle[:, lanes].astype(f32) + returned).astype(bf16)


def fused_device(
    hidden_state,
    queries,
    key_cache,
    value_cache,
    lengths,
    assignment,
    out_weight,
    norm_gain,
    gate_weight,
    up_weight,
    down_weight,
):
    rows_dev, columns = hidden_state.shape
    n_att, n_ffn = lax.axis_size("att"), lax.axis_size("ffn")
    requests = rows_dev * n_att
    kv_total, group_rows, _ = out_weight.shape
    kv_local = kv_total // n_ffn
    head = key_cache.shape[1] // kv_local
    per_group = queries.shape[1] // (kv_local * head)
    heads_here = group_rows // head
    pool = key_cache.shape[0]
    hidden_units = gate_weight.shape[0]
    units = hidden_units // n_ffn
    pad = -(-rows_dev // 16) * 16
    padded = n_att * pad
    i32, bf16, f32 = jnp.int32, jnp.bfloat16, jnp.float32

    own_slots = lax.dynamic_slice_in_dim(assignment, lax.axis_index("att") * rows_dev, rows_dev)
    k_ix = jnp.arange(kv_local, dtype=i32)
    g_ix = jnp.arange(per_group, dtype=i32)
    s_ix = jnp.arange(rows_dev, dtype=i32)
    a_ix = jnp.arange(n_att, dtype=i32)
    h_ix = jnp.arange(heads_here, dtype=i32)
    query_at = (
        own_slots[None, :, None] * (kv_local * per_group)
        + k_ix[:, None, None] * per_group
        + g_ix[None, None, :]
    ).reshape(-1)
    starts = jnp.sum(jnp.where(s_ix[None, :] < s_ix[:, None], lengths[None, :], 0), axis=1)
    first = jnp.repeat(starts, per_group)
    count = jnp.repeat(lengths, per_group)
    spread_at = (
        k_ix[None, :, None, None] * (rows_dev * per_group)
        + s_ix[None, None, None, :] * per_group
        + a_ix[:, None, None, None] * heads_here
        + h_ix[None, None, :, None]
    ).reshape(-1)
    all_ix = jnp.arange(requests, dtype=i32)
    inverse = jnp.sum(
        jnp.where(assignment[None, :] == all_ix[:, None], all_ix[None, :], 0), axis=1
    )
    inverse_pad = jnp.pad(
        inverse.reshape(n_att, rows_dev), ((0, 0), (0, pad - rows_dev)), constant_values=-1
    ).reshape(-1)
    slot_at = (inverse_pad // rows_dev) * (kv_local * heads_here * rows_dev) + inverse_pad % rows_dev
    parts = jnp.arange(kv_local * heads_here, dtype=i32)
    request_at = jnp.where(
        inverse_pad[None, :] >= 0, slot_at[None, :] + parts[:, None] * rows_dev, -1
    ).reshape(-1)
    narrow_at = (a_ix[:, None] * pad + s_ix[None, :]).reshape(-1)
    p_ix = jnp.arange(pad, dtype=i32)
    widen_at = jnp.where(
        p_ix[None, :] < rows_dev, a_ix[:, None] * rows_dev + p_ix[None, :], -1
    ).reshape(-1)
    named = [
        ("query", query_at),
        ("first", first),
        ("count", count),
        ("spread", spread_at),
        ("request", request_at),
        ("narrow", narrow_at),
        ("widen", widen_at),
    ]
    longest = max(array.shape[0] for _, array in named)
    places = {name: (n, array.shape[0]) for n, (name, array) in enumerate(named)}
    index = jnp.stack([jnp.pad(array, (0, longest - array.shape[0])) for _, array in named], axis=1)

    query_rows = queries.reshape(-1, head)
    hidden_pad = jnp.pad(hidden_state, ((0, pad - rows_dev), (0, 0)))
    piece_rows = kv_local * heads_here * rows_dev
    wide = tile_of(columns, 512)
    chunks = columns // wide
    sizes = (n_att, n_ffn, rows_dev, pad, kv_local, per_group, head)
    vmem = pl.BlockSpec(memory_space=pltpu.VMEM)
    hbm = pl.BlockSpec(memory_space=pl.ANY)
    dma = pltpu.SemaphoreType.DMA
    V = pltpu.VMEM
    flops = 2 * requests * columns * (3 * hidden_units + kv_total * group_rows)
    moved = 2 * columns * (3 * hidden_units + kv_total * group_rows) + 4 * key_cache.size
    result = pl.pallas_call(
        functools.partial(layer_kernel, sizes, places),
        out_shape=jax.ShapeDtypeStruct((pad, columns), bf16),
        in_specs=[vmem] * 4 + [hbm] * 6,
        out_specs=vmem,
        scratch_shapes=[
            V(key_cache.shape, bf16),
            V(value_cache.shape, bf16),
            V((kv_total * group_rows, columns), bf16),
            V(gate_weight.shape, bf16),
            V(up_weight.shape, bf16),
            V((n_att,) + query_rows.shape, bf16),
            V((n_att, piece_rows, head), bf16),
            V((n_att, piece_rows, head), bf16),
            V((n_ffn, n_att, piece_rows, head), bf16),
            V((padded, kv_total * group_rows), bf16),
            V((n_att, pad, columns), bf16),
            V((n_att - 1, pad, columns), bf16),
            V((pad, columns), bf16),
            V((n_att, pad, columns), bf16),
            V((requests, columns), bf16),
            V((pad, 128), f32),
            V((n_ffn - 1, pad, 128), f32),
            V((pad, 128), f32),
            V((n_att, pad, 128), f32),
            V((n_ffn - 1, 2, requests, units), bf16),
            V((n_ffn - 1, 2, requests, units), bf16),
            V((n_ffn, requests, units), bf16),
            V((requests, columns), f32),
            dma((2 + kv_total,)),
            dma((2, n_ffn)),
            dma((n_ffn,)),
            dma((4, n_att - 1)),
            dma((4, n_att - 1)),
            dma((4, n_ffn - 1)),
            dma((4, n_ffn - 1)),
            dma((n_att - 1, chunks)),
            dma((n_att - 1, chunks)),
            dma((n_att - 1, chunks)),
            dma((n_att - 1, chunks)),
        ],
        compiler_params=pltpu.CompilerParams(
            collective_id=0, has_side_effects=True, vmem_limit_bytes=61 * 2**20
        ),
        cost_estimate=pl.CostEstimate(flops=flops, bytes_accessed=moved, transcendentals=0),
        name="decode_layer",
    )(
        query_rows,
        hidden_pad,
        norm_gain[None, :],
        index,
        key_cache,
        value_cache,
        out_weight,
        gate_weight,
        up_weight,
        down_weight,
    )
    return result[:rows_dev]


def fits_kernel(mesh, out_weight, key_cache, gate_weight):
    n_att, n_ffn = mesh.shape["att"], mesh.shape["ffn"]
    head = key_cache.shape[1] // out_weight.shape[0]
    group_rows = out_weight.shape[1] // n_att
    units = gate_weight.shape[0] // (n_att * n_ffn)
    return n_ffn & (n_ffn - 1) == 0 and group_rows % head == 0 and units % 128 == 0


def solution(mesh):
    in_specs = (
        P(("group", "att"), "ffn"),
        P(("group", "att"), "ffn"),
        P(("group", "att"), "ffn"),
        P(("group", "att"), "ffn"),
        P(("group", "att")),
        P("group"),
        P(None, "att", "ffn"),
        P("ffn"),
        P("att", "ffn"),
        P("att", "ffn"),
        P("att", "ffn"),
    )
    out_specs = P(("group", "att"), "ffn")

    def run(*arrays):
        body = fused_device if fits_kernel(mesh, arrays[6], arrays[2], arrays[8]) else per_device
        return jax.shard_map(
            body, mesh=mesh, in_specs=in_specs, out_specs=out_specs, check_vma=False
        )(*arrays)

    return run
```
